32 devices in a mesh: grp: 2 (over y), bl: 4 (over z), ch: 2 (over x), pol: 2 (over core).
Axes of the slice: x: 2, y: 2, z: 4, core: 2. Of those that a mesh axis runs over, the one named last changes fastest.
Arguments:
- visibilities: float32 [2, 2, 256, 2048], P(None, 'pol', 'ch', ('grp', 'bl')), parts along dimension 3
- beam: float32 [16, 2, 2, 256, 512], P('grp', None, 'pol', 'ch', 'bl'), parts along dimension 0, may hold values from -1.4 to 1.4, as said below
- coherency: float32 [16, 2, 256], P(('grp', 'bl'), 'pol', 'ch'), parts along dimension 0, may hold values from 0.5 to 3, as said below
- owner: int32 [16], P('grp'), parts along dimension 0, may hold values from 0 to 7, as said below
- positions: float32 [2, 1024], P(None, 'grp'), parts along dimension 1, may hold values from -2 to 2
- direction_lm: float32 [16, 2], P('grp'), parts along dimension 0, may hold values from -0.3 to 0.3
- pairs: int32 [2, 2048], P(None, ('grp', 'bl')), parts along dimension 1, may hold values from 0 to 511, as said below
Outputs:
- residual: float32 [2, 2, 256, 2048], P(None, 'pol', 'ch', ('grp', 'bl')), parts along dimension 3
- gains: float32 [16, 2, 2, 512], P('grp', None, 'pol'), parts along dimension 0
The draws below stay inside these ranges and needn't reach their ends.
There are 2 independent parts, one for each index of `grp`. The reference program is written for one: setup_inputs(seed, part) draws one part's arguments, and reference() takes and returns one part's arrays. A program takes and returns all parts, laid end to end along the dimension named above; each array names one. Nothing has to cross between parts.
Inputs may be any that keep to these rules, and one draw needn't show every extreme that they name: `pairs`: each device's 2 * 128 baseline slots hold whole tiles of live baselines first, then padding; a live slot names two different stations, the first below the second; a padding slot names station 0 twice; every device has at least one live tile and some device has all slots live. `owner`: 8 different rows of the coherency table; row k is held by index k // 2 of bl. Positive coherency spectra. `beam`: beam Jones magnitudes between 0.6 and 1.4.
All inputs are finite; a program needn't handle non-finite values.
Results may differ from the reference program's by a relative error of at most 0.0001.
Values sent between devices are 32-bit elements; how exact they have to be, the bound alone decides.
A program may use at most 128 MiB of HBM per device.

```python
import math
import jax
import jax.numpy as jnp

NS = 512
NC = 256
POL = 2
DIRS = 8
ITERS = 2
TILE = 128
TILES_DEV = 2
SLOTS = 8
NB = 1024
N_BL = 4


def predict_drawn(beam_dir, flux_row, first, second, east_diff, north_diff, lm_dir, freq, live):
    left_r = beam_dir[0][:, :, first]
    left_i = beam_dir[1][:, :, first]
    right_r = beam_dir[0][:, :, second]
    right_i = beam_dir[1][:, :, second]
    cross_r = left_r * right_r + left_i * right_i
    cross_i = left_i * right_r - left_r * right_i
    phase = 2.0 * math.pi * freq[:, None] * (east_diff * lm_dir[0] + north_diff * lm_dir[1])[None, :]
    cosine = jnp.cos(phase)
    sine = jnp.sin(phase)
    scale = flux_row[:, :, None] * live[None, None, :]
    return ((cross_r * cosine - cross_i * sine) * scale, (cross_r * sine + cross_i * cosine) * scale)


def sky(key):
    keys = jax.random.split(key, 11)
    rest = jax.random.permutation(keys[0], SLOTS - 1)[:DIRS - 1]
    chosen = jnp.concatenate([rest.astype(jnp.int32), jnp.full((1,), SLOTS - 1, jnp.int32)])
    owner = jnp.take(chosen, jax.random.permutation(keys[1], DIRS)).astype(jnp.int32)
    flux = jnp.exp(jax.random.uniform(keys[2], (SLOTS, POL, NC), jnp.float32, math.log(0.5), math.log(3.0)))
    amplitude = jnp.exp(jax.random.uniform(keys[3], (DIRS, POL, NC, NS), jnp.float32, math.log(0.6), math.log(1.4)))
    angle = jax.random.uniform(keys[4], (DIRS, POL, NC, NS), jnp.float32, -math.pi, math.pi)
    beam = jnp.stack([amplitude * jnp.cos(angle), amplitude * jnp.sin(angle)], axis=1)
    positions = jax.random.uniform(keys[5], (2, NS), jnp.float32, -2.0, 2.0)
    cosines = jax.random.uniform(keys[6], (DIRS, 2), jnp.float32, -0.3, 0.3)
    block = TILE * TILES_DEV
    total = block * N_BL
    tiles = jax.random.randint(keys[7], (N_BL,), 1, TILES_DEV + 1)
    fullest = jax.random.randint(keys[8], (), 0, N_BL)
    tiles = jnp.where(jnp.arange(N_BL) == fullest, TILES_DEV, tiles)
    slot = jnp.arange(total)
    active = slot % block < tiles[slot // block] * TILE
    start = jax.random.randint(keys[9], (total,), 0, NS)
    offset = jax.random.randint(keys[10], (total,), 1, NS)
    other = (start + offset) % NS
    lower = jnp.minimum(start, other)
    upper = jnp.maximum(start, other)
    edge = slot == fullest * block
    lower = jnp.where(edge, 0, lower)
    upper = jnp.where(edge, NS - 1, upper)
    lower = jnp.where(active, lower, 0)
    upper = jnp.where(active, upper, 0)
    pairs = jnp.stack([lower, upper]).astype(jnp.int32)
    return (owner, flux, beam, positions, cosines, pairs)


def draw_owner(key, part):
    return sky(key)[0]


def draw_coherency(key, part):
    return sky(key)[1]


def draw_beam(key, part):
    return sky(key)[2]


def draw_positions(key, part):
    return sky(key)[3]


def draw_direction_lm(key, part):
    return sky(key)[4]


def draw_pairs(key, part):
    return sky(key)[5]


def draw_visibilities(key, part):
    owner, flux, beam, positions, cosines, pairs = sky(key)
    key = jax.random.fold_in(key, 7)
    keys = jax.random.split(key, 3)
    gain_amp = jnp.exp(jax.random.uniform(keys[0], (DIRS, POL, NS), jnp.float32, math.log(0.7), math.log(1.4)))
    gain_ang = jax.random.uniform(keys[1], (DIRS, POL, NS), jnp.float32, -0.6, 0.6)
    gain_r = gain_amp * jnp.cos(gain_ang)
    gain_i = gain_amp * jnp.sin(gain_ang)
    first = pairs[0]
    second = pairs[1]
    live = (first != second).astype(jnp.float32)
    freq = 1.0 + 0.5 * jnp.arange(NC).astype(jnp.float32) / NC
    east_diff = positions[0, first] - positions[0, second]
    north_diff = positions[1, first] - positions[1, second]
    total_r = jnp.zeros((POL, NC, NB), jnp.float32)
    total_i = jnp.zeros((POL, NC, NB), jnp.float32)
    for direction in range(DIRS):
        model_r, model_i = predict_drawn(beam[direction], flux[owner[direction]], first, second, east_diff, north_diff, cosines[direction], freq, live)
        near_r = gain_r[direction][:, first]
        near_i = gain_i[direction][:, first]
        far_r = gain_r[direction][:, second]
        far_i = gain_i[direction][:, second]
        pair_r = (near_r * far_r + near_i * far_i)[:, None, :]
        pair_i = (near_i * far_r - near_r * far_i)[:, None, :]
        total_r = total_r + pair_r * model_r - pair_i * model_i
        total_i = total_i + pair_r * model_i + pair_i * model_r
    noise = 0.3 * jax.random.normal(keys[2], (2, POL, NC, NB), jnp.float32)
    return jnp.stack([total_r, total_i]) + noise


def setup_inputs(seed: int = 0, part: int = 0) -> dict:
    key_of = jax.random.split(jax.random.key(seed), 8)
    part_splits = jax.random.split(jax.random.fold_in(key_of[7], part), 8)
    visibilities = draw_visibilities(jax.random.fold_in(jax.random.fold_in(key_of[7], part), 71), part)
    beam = draw_beam(jax.random.fold_in(jax.random.fold_in(key_of[7], part), 71), part)
    coherency = draw_coherency(jax.random.fold_in(jax.random.fold_in(key_of[7], part), 71), part)
    owner = draw_owner(jax.random.fold_in(jax.random.fold_in(key_of[7], part), 71), part)
    positions = draw_positions(jax.random.fold_in(jax.random.fold_in(key_of[7], part), 71), part)
    direction_lm = draw_direction_lm(jax.random.fold_in(jax.random.fold_in(key_of[7], part), 71), part)
    pairs = draw_pairs(jax.random.fold_in(jax.random.fold_in(key_of[7], part), 71), part)
    return dict(visibilities=visibilities, beam=beam, coherency=coherency, owner=owner, positions=positions, direction_lm=direction_lm, pairs=pairs)


MIXING = 0.5


def predict(beam_dir, flux_row, first, second, east_diff, north_diff, lm_dir, freq, live):
    left_r = beam_dir[0][:, :, first]
    left_i = beam_dir[1][:, :, first]
    right_r = beam_dir[0][:, :, second]
    right_i = beam_dir[1][:, :, second]
    cross_r = left_r * right_r + left_i * right_i
    cross_i = left_i * right_r - left_r * right_i
    phase = 2.0 * math.pi * freq[:, None] * (east_diff * lm_dir[0] + north_diff * lm_dir[1])[None, :]
    cosine = jnp.cos(phase)
    sine = jnp.sin(phase)
    scale = flux_row[:, :, None] * live[None, None, :]
    model_r = (cross_r * cosine - cross_i * sine) * scale
    model_i = (cross_r * sine + cross_i * cosine) * scale
    return model_r, model_i


def station_sums(res_r, res_i, model_r, model_i, gain_r, gain_i, first, second, stations):
    prod_r = jnp.sum(res_r * model_r + res_i * model_i, axis=1)
    prod_i = jnp.sum(res_i * model_r - res_r * model_i, axis=1)
    power = jnp.sum(model_r * model_r + model_i * model_i, axis=1)
    far_r = gain_r[:, second]
    far_i = gain_i[:, second]
    near_r = gain_r[:, first]
    near_i = gain_i[:, first]
    head_r = prod_r * far_r - prod_i * far_i
    head_i = prod_r * far_i + prod_i * far_r
    tail_r = prod_r * near_r + prod_i * near_i
    tail_i = prod_r * near_i - prod_i * near_r
    den_head = power * (far_r * far_r + far_i * far_i)
    den_tail = power * (near_r * near_r + near_i * near_i)

    def segsum(values, index):
        return jax.ops.segment_sum(values.T, index, stations).T

    return jnp.stack([segsum(head_r, first) + segsum(tail_r, second),
                      segsum(head_i, first) + segsum(tail_i, second),
                      segsum(den_head, first) + segsum(den_tail, second),
                      segsum(power, first) + segsum(power, second)])


def update_gains(sums, gain_r, gain_i):
    top_r = sums[0] + MIXING * sums[3] + 1.0
    top_i = sums[1]
    bottom = sums[2] + MIXING * sums[3] + 1.0
    return 0.5 * gain_r + 0.5 * top_r / bottom, 0.5 * gain_i + 0.5 * top_i / bottom


def subtract(res_r, res_i, model_r, model_i, gain_r, gain_i, first, second):
    near_r = gain_r[:, first]
    near_i = gain_i[:, first]
    far_r = gain_r[:, second]
    far_i = gain_i[:, second]
    pair_r = (near_r * far_r + near_i * far_i)[:, None, :]
    pair_i = (near_i * far_r - near_r * far_i)[:, None, :]
    res_r = res_r - (pair_r * model_r - pair_i * model_i)
    res_i = res_i - (pair_r * model_i + pair_i * model_r)
    return res_r, res_i


def reference(visibilities, beam, coherency, owner, positions, direction_lm, pairs):
    first = pairs[0]
    second = pairs[1]
    live = (first != second).astype(jnp.float32)
    freq = 1.0 + 0.5 * jnp.arange(NC).astype(jnp.float32) / NC
    east_diff = positions[0, first] - positions[0, second]
    north_diff = positions[1, first] - positions[1, second]
    res_r = visibilities[0]
    res_i = visibilities[1]
    stations = beam.shape[4]
    solved = []
    for direction in range(DIRS):
        model_r, model_i = predict(beam[direction], coherency[owner[direction]], first, second,
                                   east_diff, north_diff, direction_lm[direction], freq, live)
        gain_r = jnp.ones((res_r.shape[0], stations), jnp.float32)
        gain_i = jnp.zeros((res_r.shape[0], stations), jnp.float32)
        for sweep in range(ITERS):
            sums = station_sums(res_r, res_i, model_r, model_i, gain_r, gain_i, first, second, stations)
            gain_r, gain_i = update_gains(sums, gain_r, gain_i)
        res_r, res_i = subtract(res_r, res_i, model_r, model_i, gain_r, gain_i, first, second)
        solved.append(jnp.stack([gain_r, gain_i]))
    return jnp.stack([res_r, res_i]), jnp.stack(solved)
```

```python
import functools
import math

import jax
import jax.numpy as jnp
import numpy as np
from jax import lax
from jax.experimental import pallas as pl
from jax.experimental.pallas import tpu as pltpu
from jax.sharding import PartitionSpec as P

NC = 256
DIRS = 8
MIXING = 0.5
VMEM_LIMIT = 48 * 1024 * 1024


def turn_polynomials():
    x = (np.cos(np.pi * (np.arange(400) + 0.5) / 400) + 1) / 8
    root = np.sqrt(x)
    fit = np.polynomial.polynomial.Polynomial.fit
    sine = fit(x, np.sin(2 * np.pi * root) / root, 7, domain=[0, 0.25], window=[0, 0.25]).coef
    cosine = fit(x, np.cos(2 * np.pi * root), 8, domain=[0, 0.25], window=[0, 0.25]).coef
    return ([float(c) for c in sine], [float(c) for c in cosine])


SINE, COSINE = turn_polynomials()


def horner(coefs, z):
    total = jnp.full_like(z, coefs[-1])
    for c in coefs[-2::-1]:
        total = total * z + c
    return total


def phasor(turns):
    rest = turns - jnp.round(turns)
    z = rest * rest
    return horner(COSINE, z), rest * horner(SINE, z)


def row_of(d):
    return 3 * d + d * (d - 1)


ROWS = row_of(DIRS)


def terms(value, count):
    parts = []
    for _ in range(count):
        part = value.astype(jnp.bfloat16)
        parts.append(part)
        value = value - part.astype(jnp.float32)
    return parts


def look_up(value, hot, count):
    m = value.shape[0]
    out = jnp.dot(
        jnp.concatenate(terms(value, count), axis=0), hot, preferred_element_type=jnp.float32
    )
    return sum(out[k * m : (k + 1) * m] for k in range(1, count)) + out[:m]


def add_up(value, hot, count):
    m = value.shape[0]
    out = lax.dot_general(
        jnp.concatenate(terms(value, count), axis=0),
        hot,
        (((1,), (1,)), ((), ())),
        preferred_element_type=jnp.float32,
    )
    return sum(out[k * m : (k + 1) * m] for k in range(1, count)) + out[:m]


def fill_hot(pairs_ref, hot):
    stations, n = hot.shape
    nb = n // 2
    ids = lax.broadcasted_iota(jnp.int32, (stations, nb), 0)
    for side in range(2):
        hot[:, side * nb : (side + 1) * nb] = jnp.where(
            ids == pairs_ref[side : side + 1, :], 1.0, 0.0
        ).astype(jnp.bfloat16)


def model_kernel(lm_ref, beam_ref, vis_ref, flux_ref, freq_ref, pos_ref, pairs_ref, model_ref, sums_ref, hot):
    nb = pairs_ref.shape[1]
    k = freq_ref.shape[0]
    fill_hot(pairs_ref, hot)
    at = look_up(pos_ref[...], hot[...], 3)
    apart = at[:, :nb] - at[:, nb:]
    live = jnp.where(pairs_ref[0:1, :] != pairs_ref[1:2, :], 1.0, 0.0)
    freq = freq_ref[...]

    def row(value):
        return jnp.sum(value, axis=0, keepdims=True)

    for d in range(DIRS):
        turns = freq * (apart[0:1] * lm_ref[d, 0] + apart[1:2] * lm_ref[d, 1])
        cosine, sine = phasor(turns)
        e_r, e_i = beam_ref[d, 0], beam_ref[d, 1]
        both_r = look_up(e_r, hot[...], 2)
        both_i = look_up(e_i, hot[...], 2)
        left_r, right_r = both_r[:, :nb], both_r[:, nb:]
        left_i, right_i = both_i[:, :nb], both_i[:, nb:]
        cross_r = left_r * right_r + left_i * right_i
        cross_i = left_i * right_r - left_r * right_i
        scale = flux_ref[d] * live
        m_r = (cross_r * cosine - cross_i * sine) * scale
        m_i = (cross_r * sine + cross_i * cosine) * scale
        model_ref[d, 0] = m_r
        model_ref[d, 1] = m_i
        v_r, v_i = vis_ref[0], vis_ref[1]
        at_row = row_of(d)
        sums_ref[at_row : at_row + 1] = row(m_r * m_r + m_i * m_i)
        sums_ref[at_row + 1 : at_row + 2] = row(v_r * m_r + v_i * m_i)
        sums_ref[at_row + 2 : at_row + 3] = row(v_i * m_r - v_r * m_i)
        for e in range(d):
            o_r, o_i = model_ref[e, 0], model_ref[e, 1]
            b = at_row + 3 + 2 * e
            sums_ref[b : b + 1] = row(o_r * m_r + o_i * m_i)
            sums_ref[b + 1 : b + 2] = row(o_i * m_r - o_r * m_i)


def solve_kernel(pairs_ref, sums_ref, vis_ref, model_ref, res_ref, gains_ref, hot, pair):
    nb = pairs_ref.shape[1]
    fill_hot(pairs_ref, hot)
    power = jnp.concatenate([sums_ref[row_of(d) : row_of(d) + 1] for d in range(DIRS)], axis=0)
    weights = add_up(jnp.concatenate([power, power], axis=1), hot[...], 3)

    for d in range(DIRS):
        at_row = row_of(d)
        q = sums_ref[at_row : at_row + 1]
        p_r = sums_ref[at_row + 1 : at_row + 2]
        p_i = sums_ref[at_row + 2 : at_row + 3]
        for e in range(d):
            b = at_row + 3 + 2 * e
            b_r, b_i = sums_ref[b : b + 1], sums_ref[b + 1 : b + 2]
            g_r, g_i = pair[2 * e : 2 * e + 1], pair[2 * e + 1 : 2 * e + 2]
            p_r = p_r - (g_r * b_r - g_i * b_i)
            p_i = p_i - (g_r * b_i + g_i * b_r)
        w = weights[d : d + 1]
        first = add_up(
            jnp.concatenate(
                [jnp.concatenate([p_r, p_r], axis=1), jnp.concatenate([p_i, -p_i], axis=1)], axis=0
            ),
            hot[...],
            3,
        )
        scale = 0.5 / (w + MIXING * w + 1.0)
        gain_r = 0.5 + (first[0:1] + MIXING * w + 1.0) * scale
        gain_i = first[1:2] * scale
        at = look_up(jnp.concatenate([gain_r, gain_i], axis=0), hot[...], 3)
        near_r, far_r = at[0:1, :nb], at[0:1, nb:]
        near_i, far_i = at[1:2, :nb], at[1:2, nb:]
        head = [p_r * far_r - p_i * far_i, p_r * far_i + p_i * far_r, q * (far_r * far_r + far_i * far_i)]
        tail = [p_r * near_r + p_i * near_i, p_r * near_i - p_i * near_r, q * (near_r * near_r + near_i * near_i)]
        second = add_up(
            jnp.concatenate([jnp.concatenate([h, t], axis=1) for h, t in zip(head, tail)], axis=0),
            hot[...],
            3,
        )
        scale = 0.5 / (second[2:3] + MIXING * w + 1.0)
        gain_r = 0.5 * gain_r + (second[0:1] + MIXING * w + 1.0) * scale
        gain_i = 0.5 * gain_i + second[1:2] * scale
        gains = jnp.concatenate([gain_r, gain_i], axis=0)
        gains_ref[d] = gains
        at = look_up(gains, hot[...], 3)
        near_r, far_r = at[0:1, :nb], at[0:1, nb:]
        near_i, far_i = at[1:2, :nb], at[1:2, nb:]
        pair[2 * d : 2 * d + 1] = near_r * far_r + near_i * far_i
        pair[2 * d + 1 : 2 * d + 2] = near_i * far_r - near_r * far_i

    r_r, r_i = vis_ref[0], vis_ref[1]
    for d in range(DIRS):
        g_r, g_i = pair[2 * d : 2 * d + 1], pair[2 * d + 1 : 2 * d + 2]
        m_r, m_i = model_ref[d, 0], model_ref[d, 1]
        r_r = r_r - (g_r * m_r - g_i * m_i)
        r_i = r_i - (g_r * m_i + g_i * m_r)
    res_ref[0] = r_r
    res_ref[1] = r_i


def on_device(n_bl, visibilities, beam, coherency, owner, positions, direction_lm, pairs):
    chans = visibilities.shape[2]
    k = chans // n_bl
    stations = positions.shape[1]
    nb = pairs.shape[1] * n_bl
    start = lax.axis_index("ch") * chans + lax.axis_index("bl") * k
    freq = 1.0 + 0.5 * (start + jnp.arange(k)).astype(jnp.float32)[:, None] / NC
    all_pairs = lax.all_gather(pairs, "bl", axis=1, tiled=True)
    e = lax.all_to_all(beam[:, :, 0], "bl", split_axis=2, concat_axis=3, tiled=True)
    v = lax.all_to_all(visibilities[:, 0], "bl", split_axis=1, concat_axis=2, tiled=True)
    table = lax.all_to_all(coherency[:, 0], "bl", split_axis=1, concat_axis=0, tiled=True)
    flux = table[owner][:, :, None]
    vmem = pl.BlockSpec(memory_space=pltpu.VMEM)
    model, sums = pl.pallas_call(
        model_kernel,
        out_shape=(
            jax.ShapeDtypeStruct((DIRS, 2, k, nb), jnp.float32),
            jax.ShapeDtypeStruct((ROWS, nb), jnp.float32),
        ),
        in_specs=[pl.BlockSpec(memory_space=pltpu.SMEM)] + [vmem] * 6,
        out_specs=(vmem, vmem),
        scratch_shapes=[pltpu.VMEM((stations, 2 * nb), jnp.bfloat16)],
        compiler_params=pltpu.CompilerParams(vmem_limit_bytes=VMEM_LIMIT),
        name="model",
    )(direction_lm, e, v, flux, freq, positions, all_pairs)
    sums = lax.psum(sums, ("bl", "ch"))
    res, gains = pl.pallas_call(
        solve_kernel,
        out_shape=(
            jax.ShapeDtypeStruct((2, k, nb), jnp.float32),
            jax.ShapeDtypeStruct((DIRS, 2, stations), jnp.float32),
        ),
        in_specs=[vmem] * 4,
        out_specs=(vmem, vmem),
        scratch_shapes=[
            pltpu.VMEM((stations, 2 * nb), jnp.bfloat16),
            pltpu.VMEM((2 * DIRS, nb), jnp.float32),
        ],
        compiler_params=pltpu.CompilerParams(vmem_limit_bytes=VMEM_LIMIT),
        name="solve",
    )(all_pairs, sums, v, model)
    res = lax.all_to_all(res, "bl", split_axis=2, concat_axis=1, tiled=True)
    return (res[:, None], gains[:, :, None])


def solution(mesh):
    return jax.shard_map(
        functools.partial(on_device, mesh.shape["bl"]),
        mesh=mesh,
        in_specs=(
            P(None, "pol", "ch", ("grp", "bl")),
            P("grp", None, "pol", "ch", "bl"),
            P(("grp", "bl"), "pol", "ch"),
            P("grp"),
            P(None, "grp"),
            P("grp", None),
            P(None, ("grp", "bl")),
        ),
        out_specs=(P(None, "pol", "ch", ("grp", "bl")), P("grp", None, "pol", None)),
        check_vma=False,
    )
```

```python
import functools
import math

import jax
import jax.numpy as jnp
import numpy as np
from jax import lax
from jax.experimental import pallas as pl
from jax.experimental.pallas import tpu as pltpu
from jax.sharding import PartitionSpec as P

NC = 256
DIRS = 8
MIXING = 0.5
VMEM_LIMIT = 48 * 1024 * 1024


def turn_polynomials():
    x = (np.cos(np.pi * (np.arange(400) + 0.5) / 400) + 1) / 8
    root = np.sqrt(x)
    fit = np.polynomial.polynomial.Polynomial.fit
    sine = fit(x, np.sin(2 * np.pi * root) / root, 7, domain=[0, 0.25], window=[0, 0.25]).coef
    cosine = fit(x, np.cos(2 * np.pi * root), 8, domain=[0, 0.25], window=[0, 0.25]).coef
    return ([float(c) for c in sine], [float(c) for c in cosine])


SINE, COSINE = turn_polynomials()


def horner(coefs, z):
    total = jnp.full_like(z, coefs[-1])
    for c in coefs[-2::-1]:
        total = total * z + c
    return total


def phasor(turns):
    rest = turns - jnp.round(turns)
    z = rest * rest
    return horner(COSINE, z), rest * horner(SINE, z)


def row_of(d):
    return 3 * d + d * (d - 1)


ROWS = row_of(DIRS)


def terms(value, count):
    parts = []
    for _ in range(count):
        part = value.astype(jnp.bfloat16)
        parts.append(part)
        value = value - part.astype(jnp.float32)
    return parts


def look_up(value, hot, count):
    m = value.shape[0]
    out = jnp.dot(
        jnp.concatenate(terms(value, count), axis=0), hot, preferred_element_type=jnp.float32
    )
    return sum(out[k * m : (k + 1) * m] for k in range(1, count)) + out[:m]


def add_up(value, hot, count):
    m = value.shape[0]
    out = lax.dot_general(
        jnp.concatenate(terms(value, count), axis=0),
        hot,
        (((1,), (1,)), ((), ())),
        preferred_element_type=jnp.float32,
    )
    return sum(out[k * m : (k + 1) * m] for k in range(1, count)) + out[:m]


def one_kernel(
    n_bl, n_ch,
    lm_ref, owner_ref, freq_ref, pos_ref, pairs_ref, coh_ref, vis_ref, beam_ref,
    res_ref, gains_ref,
    pairs_in, coh_in, vis_in, beam_in, hot, model, part, part_in, total, full, pair, res_out, res_in,
    ex_send, ex_recv, sum_send, sum_recv, all_send, all_recv, back_send, back_recv,
):
    k = freq_ref.shape[0]
    nb_loc = pairs_ref.shape[1]
    nb = nb_loc * n_bl
    n = n_bl * n_ch
    rp = total.shape[0]
    stations = pos_ref.shape[1]
    slot_dev = coh_ref.shape[1]
    my_bl, my_ch = lax.axis_index("bl"), lax.axis_index("ch")
    me = my_bl * n_ch + my_ch

    def peer(off):
        return lax.rem(me + off, n)

    def place(p):
        return {"bl": lax.div(p, n_ch), "ch": lax.rem(p, n_ch)}

    barrier = pltpu.get_barrier_semaphore()

    def greet(off, _):
        pl.semaphore_signal(barrier, inc=1, device_id=place(peer(off)), device_id_type=pl.DeviceIdType.MESH)
        return 0

    lax.fori_loop(1, n, greet, 0)
    pl.semaphore_wait(barrier, n - 1)

    def source(kind, to):
        if kind == 0:
            return pairs_ref
        if kind == 1:
            return coh_ref.at[to]
        if kind == 2:
            return vis_ref.at[:, to]
        return beam_ref.at[kind - 3, :, to]

    def landing(kind, frm):
        if kind == 0:
            return pairs_in.at[frm]
        if kind == 1:
            return coh_in.at[frm]
        if kind == 2:
            return vis_in.at[frm]
        return beam_in.at[kind - 3, frm]

    def own(kind):
        return pltpu.make_async_copy(source(kind, my_bl), landing(kind, my_bl), ex_recv.at[kind, my_bl])

    def exchange(kind, to, frm):
        return pltpu.make_async_remote_copy(
            src_ref=source(kind, to),
            dst_ref=landing(kind, frm),
            send_sem=ex_send.at[kind, to],
            recv_sem=ex_recv.at[kind, frm],
            device_id={"bl": to},
            device_id_type=pl.DeviceIdType.MESH,
        )

    kinds = 3 + DIRS
    for kind in range(kinds):
        for off in range(1, n_bl):
            exchange(kind, lax.rem(my_bl + off, n_bl), my_bl).start()
        own(kind).start()

    def arrived(kind):
        own(kind).wait()
        for off in range(1, n_bl):
            frm = lax.rem(my_bl + n_bl - off, n_bl)
            exchange(kind, frm, frm).wait_recv()

    arrived(0)
    ids = lax.broadcasted_iota(jnp.int32, (stations, nb_loc), 0)
    live_parts = []
    for frm in range(n_bl):
        for side in range(2):
            at = side * nb + frm * nb_loc
            hot[:, at : at + nb_loc] = jnp.where(
                ids == pairs_in[frm, side : side + 1, :], 1.0, 0.0
            ).astype(jnp.bfloat16)
        live_parts.append(
            jnp.where(pairs_in[frm, 0:1, :] != pairs_in[frm, 1:2, :], 1.0, 0.0)
        )
    live = jnp.concatenate(live_parts, axis=1)
    at = look_up(pos_ref[...], hot[...], 3)
    apart = at[:, :nb] - at[:, nb:]
    freq = freq_ref[...]
    eye = lax.broadcasted_iota(jnp.int32, (k, k), 0) == lax.broadcasted_iota(jnp.int32, (k, k), 1)

    def put_row(r, value):
        line = jnp.sum(value, axis=0, keepdims=True)
        c, i = r // rp, r % rp
        for j in range(n_bl):
            part[j, c, i : i + 1, :] = line[:, j * nb_loc : (j + 1) * nb_loc]

    def get_row(r):
        c, i = r // rp, r % rp
        return jnp.concatenate([full[j, c, i : i + 1, :] for j in range(n_bl)], axis=1)

    if n_ch * rp > ROWS:
        part[...] = jnp.zeros_like(part)
    arrived(1)
    arrived(2)
    vis = [jnp.concatenate([vis_in[frm, c] for frm in range(n_bl)], axis=1) for c in range(2)]
    for d in range(DIRS):
        turns = freq * (apart[0:1] * lm_ref[d, 0] + apart[1:2] * lm_ref[d, 1])
        cosine, sine = phasor(turns)
        line = jnp.zeros((1, k), jnp.float32)
        for r in range(n_bl * slot_dev):
            line = line + jnp.where(
                owner_ref[d] == r, coh_in[r // slot_dev, r % slot_dev : r % slot_dev + 1, :], 0.0
            )
        flux = jnp.sum(jnp.where(eye, line, 0.0), axis=1, keepdims=True)
        scale = flux * live
        arrived(3 + d)
        e = jnp.concatenate(
            [
                jnp.concatenate([beam_in[d, frm, c] for frm in range(n_bl)], axis=1)
                for c in range(2)
            ],
            axis=0,
        )
        both = look_up(e, hot[...], 2)
        left_r, right_r = both[:k, :nb], both[:k, nb:]
        left_i, right_i = both[k:, :nb], both[k:, nb:]
        cross_r = left_r * right_r + left_i * right_i
        cross_i = left_i * right_r - left_r * right_i
        m_r = (cross_r * cosine - cross_i * sine) * scale
        m_i = (cross_r * sine + cross_i * cosine) * scale
        model[d, 0] = m_r
        model[d, 1] = m_i
        at_row = row_of(d)
        put_row(at_row, m_r * m_r + m_i * m_i)
        put_row(at_row + 1, vis[0] * m_r + vis[1] * m_i)
        put_row(at_row + 2, vis[1] * m_r - vis[0] * m_i)
        for f in range(d):
            o_r, o_i = model[f, 0], model[f, 1]
            put_row(at_row + 3 + 2 * f, o_r * m_r + o_i * m_i)
            put_row(at_row + 4 + 2 * f, o_i * m_r - o_r * m_i)

    def share(p, slot):
        return pltpu.make_async_remote_copy(
            src_ref=part.at[lax.div(p, n_ch), lax.rem(p, n_ch)],
            dst_ref=part_in.at[slot],
            send_sem=sum_send.at[p],
            recv_sem=sum_recv.at[slot],
            device_id=place(p),
            device_id_type=pl.DeviceIdType.MESH,
        )

    def spread(p, slot):
        return pltpu.make_async_remote_copy(
            src_ref=total,
            dst_ref=full.at[lax.div(slot, n_ch), lax.rem(slot, n_ch)],
            send_sem=all_send.at[p],
            recv_sem=all_recv.at[slot],
            device_id=place(p),
            device_id_type=pl.DeviceIdType.MESH,
        )

    def each(body):
        def step(off, _):
            body(peer(off))
            return 0

        lax.fori_loop(1, n, step, 0)

    each(lambda p: share(p, me).start())
    part_in[me] = part[my_bl, my_ch]
    each(lambda p: share(p, p).wait_recv())
    total[...] = lax.fori_loop(1, n, lambda s, acc: acc + part_in[s], part_in[0])
    each(lambda p: spread(p, me).start())
    full[my_bl, my_ch] = total[...]
    each(lambda p: spread(p, p).wait_recv())

    power = jnp.concatenate([get_row(row_of(d)) for d in range(DIRS)], axis=0)
    weights = add_up(jnp.concatenate([power, power], axis=1), hot[...], 3)
    for d in range(DIRS):
        at_row = row_of(d)
        q, p_r, p_i = get_row(at_row), get_row(at_row + 1), get_row(at_row + 2)
        for f in range(d):
            b_r, b_i = get_row(at_row + 3 + 2 * f), get_row(at_row + 4 + 2 * f)
            g_r, g_i = pair[2 * f : 2 * f + 1], pair[2 * f + 1 : 2 * f + 2]
            p_r = p_r - (g_r * b_r - g_i * b_i)
            p_i = p_i - (g_r * b_i + g_i * b_r)
        w = weights[d : d + 1]
        first = add_up(
            jnp.concatenate(
                [jnp.concatenate([p_r, p_r], axis=1), jnp.concatenate([p_i, -p_i], axis=1)], axis=0
            ),
            hot[...],
            3,
        )
        scale = 0.5 / (w + MIXING * w + 1.0)
        gain_r = 0.5 + (first[0:1] + MIXING * w + 1.0) * scale
        gain_i = first[1:2] * scale
        at = look_up(jnp.concatenate([gain_r, gain_i], axis=0), hot[...], 3)
        near_r, far_r = at[0:1, :nb], at[0:1, nb:]
        near_i, far_i = at[1:2, :nb], at[1:2, nb:]
        head = [p_r * far_r - p_i * far_i, p_r * far_i + p_i * far_r, q * (far_r * far_r + far_i * far_i)]
        tail = [p_r * near_r + p_i * near_i, p_r * near_i - p_i * near_r, q * (near_r * near_r + near_i * near_i)]
        second = add_up(
            jnp.concatenate([jnp.concatenate([h, t], axis=1) for h, t in zip(head, tail)], axis=0),
            hot[...],
            3,
        )
        scale = 0.5 / (second[2:3] + MIXING * w + 1.0)
        gain_r = 0.5 * gain_r + (second[0:1] + MIXING * w + 1.0) * scale
        gain_i = 0.5 * gain_i + second[1:2] * scale
        gains = jnp.concatenate([gain_r, gain_i], axis=0)
        gains_ref[d] = gains
        at = look_up(gains, hot[...], 3)
        near_r, far_r = at[0:1, :nb], at[0:1, nb:]
        near_i, far_i = at[1:2, :nb], at[1:2, nb:]
        pair[2 * d : 2 * d + 1] = near_r * far_r + near_i * far_i
        pair[2 * d + 1 : 2 * d + 2] = near_i * far_r - near_r * far_i

    for j in range(n_bl):
        lo, hi = j * nb_loc, (j + 1) * nb_loc
        r_r, r_i = vis_in[j, 0], vis_in[j, 1]
        for d in range(DIRS):
            g_r, g_i = pair[2 * d : 2 * d + 1, lo:hi], pair[2 * d + 1 : 2 * d + 2, lo:hi]
            m_r, m_i = model[d, 0, :, lo:hi], model[d, 1, :, lo:hi]
            r_r = r_r - (g_r * m_r - g_i * m_i)
            r_i = r_i - (g_r * m_i + g_i * m_r)
        res_out[j, 0] = r_r
        res_out[j, 1] = r_i

    def back(to, slot):
        return pltpu.make_async_remote_copy(
            src_ref=res_out.at[to],
            dst_ref=res_in.at[slot],
            send_sem=back_send.at[to],
            recv_sem=back_recv.at[slot],
            device_id={"bl": to},
            device_id_type=pl.DeviceIdType.MESH,
        )

    for off in range(1, n_bl):
        back(lax.rem(my_bl + off, n_bl), my_bl).start()
    res_in[my_bl] = res_out[my_bl]
    for off in range(1, n_bl):
        frm = lax.rem(my_bl + n_bl - off, n_bl)
        back(frm, frm).wait_recv()
    for j in range(n_bl):
        for c in range(2):
            res_ref[c, j] = res_in[j, c]

    for kind in range(kinds):
        for off in range(1, n_bl):
            to = lax.rem(my_bl + off, n_bl)
            exchange(kind, to, to).wait_send()
    each(lambda p: share(p, p).wait_send())
    each(lambda p: spread(p, p).wait_send())
    for off in range(1, n_bl):
        to = lax.rem(my_bl + off, n_bl)
        back(to, to).wait_send()


def on_device(n_bl, n_ch, visibilities, beam, coherency, owner, positions, direction_lm, pairs):
    chans = visibilities.shape[2]
    k = chans // n_bl
    stations = positions.shape[1]
    st_loc = beam.shape[4]
    nb_loc = pairs.shape[1]
    nb = nb_loc * n_bl
    slot_dev = coherency.shape[0]
    n = n_bl * n_ch
    rp = -(-ROWS // n_ch)
    start = lax.axis_index("ch") * chans + lax.axis_index("bl") * k
    freq = 1.0 + 0.5 * (start + jnp.arange(k)).astype(jnp.float32)[:, None] / NC
    coh = coherency[:, 0].reshape(slot_dev, n_bl, k).transpose(1, 0, 2)
    vis = visibilities.reshape(2, n_bl, k, nb_loc)
    beams = beam.reshape(DIRS, 2, n_bl, k, st_loc)
    vmem = pl.BlockSpec(memory_space=pltpu.VMEM)
    smem = pl.BlockSpec(memory_space=pltpu.SMEM)
    anywhere = pl.BlockSpec(memory_space=pl.ANY)
    f32 = jnp.float32
    dma = pltpu.SemaphoreType.DMA
    res, gains = pl.pallas_call(
        functools.partial(one_kernel, n_bl, n_ch),
        out_shape=(
            jax.ShapeDtypeStruct((2, n_bl, k, nb_loc), f32),
            jax.ShapeDtypeStruct((DIRS, 2, stations), f32),
        ),
        in_specs=[smem, smem, vmem, vmem, vmem, vmem, anywhere, anywhere],
        out_specs=(vmem, vmem),
        scratch_shapes=[
            pltpu.VMEM((n_bl, 2, nb_loc), jnp.int32),
            pltpu.VMEM((n_bl, slot_dev, k), f32),
            pltpu.VMEM((n_bl, 2, k, nb_loc), f32),
            pltpu.VMEM((DIRS, n_bl, 2, k, st_loc), f32),
            pltpu.VMEM((stations, 2 * nb), jnp.bfloat16),
            pltpu.VMEM((DIRS, 2, k, nb), f32),
            pltpu.VMEM((n_bl, n_ch, rp, nb_loc), f32),
            pltpu.VMEM((n, rp, nb_loc), f32),
            pltpu.VMEM((rp, nb_loc), f32),
            pltpu.VMEM((n_bl, n_ch, rp, nb_loc), f32),
            pltpu.VMEM((2 * DIRS, nb), f32),
            pltpu.VMEM((n_bl, 2, k, nb_loc), f32),
            pltpu.VMEM((n_bl, 2, k, nb_loc), f32),
            dma((3 + DIRS, n_bl)),
            dma((3 + DIRS, n_bl)),
            dma((n,)),
            dma((n,)),
            dma((n,)),
            dma((n,)),
            dma((n_bl,)),
            dma((n_bl,)),
        ],
        compiler_params=pltpu.CompilerParams(
            collective_id=0, has_side_effects=True, vmem_limit_bytes=VMEM_LIMIT
        ),
        name="peel",
    )(direction_lm, owner, freq, positions, pairs, coh, vis, beams)
    return (res.reshape(2, 1, chans, nb_loc), gains[:, :, None])


def solution(mesh):
    return jax.shard_map(
        functools.partial(on_device, mesh.shape["bl"], mesh.shape["ch"]),
        mesh=mesh,
        in_specs=(
            P(None, "pol", "ch", ("grp", "bl")),
            P("grp", None, "pol", "ch", "bl"),
            P(("grp", "bl"), "pol", "ch"),
            P("grp"),
            P(None, "grp"),
            P("grp", None),
            P(None, ("grp", "bl")),
        ),
        out_specs=(P(None, "pol", "ch", ("grp", "bl")), P("grp", None, "pol", None)),
        check_vma=False,
    )
```

```python
import functools
import math

import jax
import jax.numpy as jnp
import numpy as np
from jax import lax
from jax.experimental import pallas as pl
from jax.experimental.pallas import tpu as pltpu
from jax.sharding import PartitionSpec as P

NC = 256
DIRS = 8
MIXING = 0.5
WINDOW = 4
VMEM_LIMIT = 48 * 1024 * 1024


def turn_polynomials():
    x = (np.cos(np.pi * (np.arange(400) + 0.5) / 400) + 1) / 8
    root = np.sqrt(x)
    fit = np.polynomial.polynomial.Polynomial.fit
    sine = fit(x, np.sin(2 * np.pi * root) / root, 7, domain=[0, 0.25], window=[0, 0.25]).coef
    cosine = fit(x, np.cos(2 * np.pi * root), 8, domain=[0, 0.25], window=[0, 0.25]).coef
    return ([float(c) for c in sine], [float(c) for c in cosine])


SINE, COSINE = turn_polynomials()


def horner(coefs, z):
    total = jnp.full_like(z, coefs[-1])
    for c in coefs[-2::-1]:
        total = total * z + c
    return total


def phasor(turns):
    rest = turns - jnp.round(turns)
    z = rest * rest
    return horner(COSINE, z), rest * horner(SINE, z)


def terms(value, count):
    parts = []
    for _ in range(count):
        part = value.astype(jnp.bfloat16)
        parts.append(part)
        value = value - part.astype(jnp.float32)
    return parts


def look_up(value, hot, count):
    m = value.shape[0]
    out = jnp.dot(
        jnp.concatenate(terms(value, count), axis=0), hot, preferred_element_type=jnp.float32
    )
    return sum(out[k * m : (k + 1) * m] for k in range(1, count)) + out[:m]


def add_up(value, hot, count):
    m = value.shape[0]
    out = lax.dot_general(
        jnp.concatenate(terms(value, count), axis=0),
        hot,
        (((1,), (1,)), ((), ())),
        preferred_element_type=jnp.float32,
    )
    return sum(out[k * m : (k + 1) * m] for k in range(1, count)) + out[:m]


def one_kernel(
    n_bl, n_ch,
    lm_ref, owner_ref, freq_ref, pos_ref, pairs_ref, coh_ref, vis_ref, beam_ref,
    res_ref, gains_ref,
    pairs_in, coh_in, vis_in, beam_in, hot, model, part, part_in, total, full, pair, res_out, res_in,
    ex_send, ex_recv, sum_send, sum_recv, all_send, all_recv, back_send, back_recv,
):
    k = freq_ref.shape[0]
    nb_loc = pairs_ref.shape[1]
    nb = nb_loc * n_bl
    n = n_bl * n_ch
    stations = pos_ref.shape[1]
    slot_dev = coh_ref.shape[1]
    my_bl, my_ch = lax.axis_index("bl"), lax.axis_index("ch")
    me = my_bl * n_ch + my_ch

    def peer(off):
        return lax.rem(me + off, n)

    def place(p):
        return {"bl": lax.div(p, n_ch), "ch": lax.rem(p, n_ch)}

    barrier = pltpu.get_barrier_semaphore()

    def greet(off, _):
        pl.semaphore_signal(barrier, inc=1, device_id=place(peer(off)), device_id_type=pl.DeviceIdType.MESH)
        return 0

    lax.fori_loop(1, n, greet, 0)
    pl.semaphore_wait(barrier, n - 1)

    def source(kind, to):
        if kind == 0:
            return pairs_ref
        if kind == 1:
            return coh_ref.at[to]
        if kind == 2:
            return vis_ref.at[:, to]
        return beam_ref.at[kind - 3, :, to]

    def landing(kind, frm):
        if kind == 0:
            return pairs_in.at[frm]
        if kind == 1:
            return coh_in.at[frm]
        if kind == 2:
            return vis_in.at[frm]
        return beam_in.at[kind - 3, frm]

    def own(kind):
        return pltpu.make_async_copy(source(kind, my_bl), landing(kind, my_bl), ex_recv.at[kind, my_bl])

    def exchange(kind, to, frm):
        return pltpu.make_async_remote_copy(
            src_ref=source(kind, to),
            dst_ref=landing(kind, frm),
            send_sem=ex_send.at[kind, to],
            recv_sem=ex_recv.at[kind, frm],
            device_id={"bl": to},
            device_id_type=pl.DeviceIdType.MESH,
        )

    kinds = 3 + DIRS

    def send_out(kind):
        for off in range(1, n_bl):
            exchange(kind, lax.rem(my_bl + off, n_bl), my_bl).start()
        own(kind).start()

    for kind in range(3 + WINDOW):
        send_out(kind)

    def arrived(kind):
        own(kind).wait()
        for off in range(1, n_bl):
            frm = lax.rem(my_bl + n_bl - off, n_bl)
            exchange(kind, frm, frm).wait_recv()

    arrived(0)
    ids = lax.broadcasted_iota(jnp.int32, (stations, nb_loc), 0)
    live_parts = []
    for frm in range(n_bl):
        for side in range(2):
            at = side * nb + frm * nb_loc
            hot[:, at : at + nb_loc] = jnp.where(
                ids == pairs_in[frm, side : side + 1, :], 1.0, 0.0
            ).astype(jnp.bfloat16)
        live_parts.append(
            jnp.where(pairs_in[frm, 0:1, :] != pairs_in[frm, 1:2, :], 1.0, 0.0)
        )
    live = jnp.concatenate(live_parts, axis=1)
    at = look_up(pos_ref[...], hot[...], 3)
    apart = at[:, :nb] - at[:, nb:]
    freq = freq_ref[...]
    eye = lax.broadcasted_iota(jnp.int32, (k, k), 0) == lax.broadcasted_iota(jnp.int32, (k, k), 1)

    def put_row(d, i, value):
        line = jnp.sum(value, axis=0, keepdims=True)
        for j in range(n_bl):
            part[d][j, i : i + 1, :] = line[:, j * nb_loc : (j + 1) * nb_loc]

    def get_row(d, i):
        return jnp.concatenate([full[d][j, i : i + 1, :] for j in range(n_bl)], axis=1)

    arrived(1)
    arrived(2)
    vis = [jnp.concatenate([vis_in[frm, c] for frm in range(n_bl)], axis=1) for c in range(2)]
    def make_model(d):
        turns = freq * (apart[0:1] * lm_ref[d, 0] + apart[1:2] * lm_ref[d, 1])
        cosine, sine = phasor(turns)
        line = jnp.zeros((1, k), jnp.float32)
        for r in range(n_bl * slot_dev):
            line = line + jnp.where(
                owner_ref[d] == r, coh_in[r // slot_dev, r % slot_dev : r % slot_dev + 1, :], 0.0
            )
        flux = jnp.sum(jnp.where(eye, line, 0.0), axis=1, keepdims=True)
        scale = flux * live
        arrived(3 + d)
        if d + WINDOW < DIRS:
            send_out(3 + d + WINDOW)
        e = jnp.concatenate(
            [
                jnp.concatenate([beam_in[d, frm, c] for frm in range(n_bl)], axis=1)
                for c in range(2)
            ],
            axis=0,
        )
        both = look_up(e, hot[...], 2)
        left_r, right_r = both[:k, :nb], both[:k, nb:]
        left_i, right_i = both[k:, :nb], both[k:, nb:]
        cross_r = left_r * right_r + left_i * right_i
        cross_i = left_i * right_r - left_r * right_i
        m_r = (cross_r * cosine - cross_i * sine) * scale
        m_i = (cross_r * sine + cross_i * cosine) * scale
        model[d, 0] = m_r
        model[d, 1] = m_i
        put_row(d, 0, m_r * m_r + m_i * m_i)
        put_row(d, 1, vis[0] * m_r + vis[1] * m_i)
        put_row(d, 2, vis[1] * m_r - vis[0] * m_i)
        for f in range(d):
            o_r, o_i = model[f, 0], model[f, 1]
            put_row(d, 3 + 2 * f, o_r * m_r + o_i * m_i)
            put_row(d, 4 + 2 * f, o_i * m_r - o_r * m_i)

    def share(d, to_bl):
        owner = to_bl * n_ch + d % n_ch
        slot = lax.rem(me - owner + n, n) - 1
        return pltpu.make_async_remote_copy(
            src_ref=part[d].at[to_bl],
            dst_ref=part_in[d].at[slot],
            send_sem=sum_send.at[d],
            recv_sem=sum_recv.at[d],
            device_id={"bl": to_bl, "ch": d % n_ch},
            device_id_type=pl.DeviceIdType.MESH,
        )

    def spread(d, p):
        return pltpu.make_async_remote_copy(
            src_ref=total[d],
            dst_ref=full[d].at[my_bl],
            send_sem=all_send.at[d],
            recv_sem=all_recv.at[d],
            device_id=place(p),
            device_id_type=pl.DeviceIdType.MESH,
        )

    def wait_for(ref, count, sem):
        block = ref.at[pl.ds(0, count)]
        pltpu.make_async_copy(block, block, sem).wait()

    def start_share(d):
        for off in range(1, n_bl):
            share(d, lax.rem(my_bl + off, n_bl)).start()

        @pl.when(my_ch != d % n_ch)
        def _():
            share(d, my_bl).start()

    def reduce_and_spread(d):
        @pl.when(my_ch == d % n_ch)
        def _():
            wait_for(part_in[d], n - 1, sum_recv.at[d])
            value = jnp.sum(part_in[d][...], axis=0) + part[d][my_bl]
            total[d][...] = value

            def step(off, _):
                spread(d, peer(off)).start()
                return 0

            lax.fori_loop(1, n, step, 0)
            full[d][my_bl] = value

    def sums_arrived(d):
        @pl.when(my_ch == d % n_ch)
        def _():
            if n_bl > 1:
                wait_for(full[d], n_bl - 1, all_recv.at[d])

        @pl.when(my_ch != d % n_ch)
        def _():
            wait_for(full[d], n_bl, all_recv.at[d])

    def sums_sent(d):
        @pl.when(my_ch == d % n_ch)
        def _():
            if n_bl > 1:
                wait_for(part[d], n_bl - 1, sum_send.at[d])
            wait_for(part_in[d], n - 1, all_send.at[d])

        @pl.when(my_ch != d % n_ch)
        def _():
            wait_for(part[d], n_bl, sum_send.at[d])

    def solve(d):
        sums_arrived(d)
        q, p_r, p_i = get_row(d, 0), get_row(d, 1), get_row(d, 2)
        for f in range(d):
            b_r, b_i = get_row(d, 3 + 2 * f), get_row(d, 4 + 2 * f)
            g_r, g_i = pair[2 * f : 2 * f + 1], pair[2 * f + 1 : 2 * f + 2]
            p_r = p_r - (g_r * b_r - g_i * b_i)
            p_i = p_i - (g_r * b_i + g_i * b_r)
        first = add_up(
            jnp.concatenate(
                [
                    jnp.concatenate([p_r, p_r], axis=1),
                    jnp.concatenate([p_i, -p_i], axis=1),
                    jnp.concatenate([q, q], axis=1),
                ],
                axis=0,
            ),
            hot[...],
            3,
        )
        w = first[2:3]
        scale = 0.5 / (w + MIXING * w + 1.0)
        gain_r = 0.5 + (first[0:1] + MIXING * w + 1.0) * scale
        gain_i = first[1:2] * scale
        at = look_up(jnp.concatenate([gain_r, gain_i], axis=0), hot[...], 3)
        near_r, far_r = at[0:1, :nb], at[0:1, nb:]
        near_i, far_i = at[1:2, :nb], at[1:2, nb:]
        head = [p_r * far_r - p_i * far_i, p_r * far_i + p_i * far_r, q * (far_r * far_r + far_i * far_i)]
        tail = [p_r * near_r + p_i * near_i, p_r * near_i - p_i * near_r, q * (near_r * near_r + near_i * near_i)]
        second = add_up(
            jnp.concatenate([jnp.concatenate([h, t], axis=1) for h, t in zip(head, tail)], axis=0),
            hot[...],
            3,
        )
        scale = 0.5 / (second[2:3] + MIXING * w + 1.0)
        gain_r = 0.5 * gain_r + (second[0:1] + MIXING * w + 1.0) * scale
        gain_i = 0.5 * gain_i + second[1:2] * scale
        gains = jnp.concatenate([gain_r, gain_i], axis=0)
        gains_ref[d] = gains
        at = look_up(gains, hot[...], 3)
        near_r, far_r = at[0:1, :nb], at[0:1, nb:]
        near_i, far_i = at[1:2, :nb], at[1:2, nb:]
        pair[2 * d : 2 * d + 1] = near_r * far_r + near_i * far_i
        pair[2 * d + 1 : 2 * d + 2] = near_i * far_r - near_r * far_i

    def take_off(j, dirs, r_r, r_i):
        lo, hi = j * nb_loc, (j + 1) * nb_loc
        for d in dirs:
            g_r, g_i = pair[2 * d : 2 * d + 1, lo:hi], pair[2 * d + 1 : 2 * d + 2, lo:hi]
            m_r, m_i = model[d, 0, :, lo:hi], model[d, 1, :, lo:hi]
            r_r = r_r - (g_r * m_r - g_i * m_i)
            r_i = r_i - (g_r * m_i + g_i * m_r)
        res_out[j, 0] = r_r
        res_out[j, 1] = r_i

    for step in range(DIRS + 1):
        if step < DIRS:
            make_model(step)
            start_share(step)
        if step >= 1:
            reduce_and_spread(step - 1)
        if step >= 2:
            solve(step - 2)
    for j in range(n_bl):
        take_off(j, range(DIRS - 1), vis_in[j, 0], vis_in[j, 1])
    solve(DIRS - 1)
    for j in range(n_bl):
        take_off(j, range(DIRS - 1, DIRS), res_out[j, 0], res_out[j, 1])

    def back(to, slot):
        return pltpu.make_async_remote_copy(
            src_ref=res_out.at[to],
            dst_ref=res_in.at[slot],
            send_sem=back_send.at[to],
            recv_sem=back_recv.at[slot],
            device_id={"bl": to},
            device_id_type=pl.DeviceIdType.MESH,
        )

    for off in range(1, n_bl):
        back(lax.rem(my_bl + off, n_bl), my_bl).start()
    res_in[my_bl] = res_out[my_bl]
    for off in range(1, n_bl):
        frm = lax.rem(my_bl + n_bl - off, n_bl)
        back(frm, frm).wait_recv()
    for j in range(n_bl):
        for c in range(2):
            res_ref[c, j] = res_in[j, c]

    for kind in range(kinds):
        for off in range(1, n_bl):
            to = lax.rem(my_bl + off, n_bl)
            exchange(kind, to, to).wait_send()
    for d in range(DIRS):
        sums_sent(d)
    for off in range(1, n_bl):
        to = lax.rem(my_bl + off, n_bl)
        back(to, to).wait_send()


def on_device(n_bl, n_ch, visibilities, beam, coherency, owner, positions, direction_lm, pairs):
    chans = visibilities.shape[2]
    k = chans // n_bl
    stations = positions.shape[1]
    st_loc = beam.shape[4]
    nb_loc = pairs.shape[1]
    nb = nb_loc * n_bl
    slot_dev = coherency.shape[0]
    n = n_bl * n_ch
    rows = [3 + 2 * d for d in range(DIRS)]
    start = lax.axis_index("ch") * chans + lax.axis_index("bl") * k
    freq = 1.0 + 0.5 * (start + jnp.arange(k)).astype(jnp.float32)[:, None] / NC
    coh = coherency[:, 0].reshape(slot_dev, n_bl, k).transpose(1, 0, 2)
    vis = visibilities.reshape(2, n_bl, k, nb_loc)
    beams = beam.reshape(DIRS, 2, n_bl, k, st_loc)
    vmem = pl.BlockSpec(memory_space=pltpu.VMEM)
    smem = pl.BlockSpec(memory_space=pltpu.SMEM)
    anywhere = pl.BlockSpec(memory_space=pl.ANY)
    f32 = jnp.float32
    dma = pltpu.SemaphoreType.DMA
    res, gains = pl.pallas_call(
        functools.partial(one_kernel, n_bl, n_ch),
        out_shape=(
            jax.ShapeDtypeStruct((2, n_bl, k, nb_loc), f32),
            jax.ShapeDtypeStruct((DIRS, 2, stations), f32),
        ),
        in_specs=[smem, smem, vmem, vmem, vmem, vmem, anywhere, anywhere],
        out_specs=(vmem, vmem),
        scratch_shapes=[
            pltpu.VMEM((n_bl, 2, nb_loc), jnp.int32),
            pltpu.VMEM((n_bl, slot_dev, k), f32),
            pltpu.VMEM((n_bl, 2, k, nb_loc), f32),
            pltpu.VMEM((DIRS, n_bl, 2, k, st_loc), f32),
            pltpu.VMEM((stations, 2 * nb), jnp.bfloat16),
            pltpu.VMEM((DIRS, 2, k, nb), f32),
            [pltpu.VMEM((n_bl, r, nb_loc), f32) for r in rows],
            [pltpu.VMEM((n - 1, r, nb_loc), f32) for r in rows],
            [pltpu.VMEM((r, nb_loc), f32) for r in rows],
            [pltpu.VMEM((n_bl, r, nb_loc), f32) for r in rows],
            pltpu.VMEM((2 * DIRS, nb), f32),
            pltpu.VMEM((n_bl, 2, k, nb_loc), f32),
            pltpu.VMEM((n_bl, 2, k, nb_loc), f32),
            dma((3 + DIRS, n_bl)),
            dma((3 + DIRS, n_bl)),
            dma((DIRS,)),
            dma((DIRS,)),
            dma((DIRS,)),
            dma((DIRS,)),
            dma((n_bl,)),
            dma((n_bl,)),
        ],
        compiler_params=pltpu.CompilerParams(
            collective_id=0, has_side_effects=True, vmem_limit_bytes=VMEM_LIMIT
        ),
        name="peel",
    )(direction_lm, owner, freq, positions, pairs, coh, vis, beams)
    return (res.reshape(2, 1, chans, nb_loc), gains[:, :, None])


def solution(mesh):
    return jax.shard_map(
        functools.partial(on_device, mesh.shape["bl"], mesh.shape["ch"]),
        mesh=mesh,
        in_specs=(
            P(None, "pol", "ch", ("grp", "bl")),
            P("grp", None, "pol", "ch", "bl"),
            P(("grp", "bl"), "pol", "ch"),
            P("grp"),
            P(None, "grp"),
            P("grp", None),
            P(None, ("grp", "bl")),
        ),
        out_specs=(P(None, "pol", "ch", ("grp", "bl")), P("grp", None, "pol", None)),
        check_vma=False,
    )
```

```python
import functools
import math

import jax
import jax.numpy as jnp
import numpy as np
from jax import lax
from jax.experimental import pallas as pl
from jax.experimental.pallas import tpu as pltpu
from jax.sharding import PartitionSpec as P

NC = 256
DIRS = 8
MIXING = 0.5
WINDOW = 4
LAG = 4
VMEM_LIMIT = 48 * 1024 * 1024


def turn_polynomials():
    x = (np.cos(np.pi * (np.arange(400) + 0.5) / 400) + 1) / 8
    root = np.sqrt(x)
    fit = np.polynomial.polynomial.Polynomial.fit
    sine = fit(x, np.sin(2 * np.pi * root) / root, 7, domain=[0, 0.25], window=[0, 0.25]).coef
    cosine = fit(x, np.cos(2 * np.pi * root), 8, domain=[0, 0.25], window=[0, 0.25]).coef
    return ([float(c) for c in sine], [float(c) for c in cosine])


SINE, COSINE = turn_polynomials()


def horner(coefs, z):
    total = jnp.full_like(z, coefs[-1])
    for c in coefs[-2::-1]:
        total = total * z + c
    return total


def phasor(turns):
    rest = turns - jnp.round(turns)
    z = rest * rest
    return horner(COSINE, z), rest * horner(SINE, z)


def terms(value, count):
    parts = []
    for _ in range(count):
        part = value.astype(jnp.bfloat16)
        parts.append(part)
        value = value - part.astype(jnp.float32)
    return parts


def look_up(value, hot, count):
    m = value.shape[0]
    out = jnp.dot(
        jnp.concatenate(terms(value, count), axis=0), hot, preferred_element_type=jnp.float32
    )
    return sum(out[k * m : (k + 1) * m] for k in range(1, count)) + out[:m]


def add_up(value, hot, count):
    m = value.shape[0]
    out = lax.dot_general(
        jnp.concatenate(terms(value, count), axis=0),
        hot,
        (((1,), (1,)), ((), ())),
        preferred_element_type=jnp.float32,
    )
    return sum(out[k * m : (k + 1) * m] for k in range(1, count)) + out[:m]


def one_kernel(
    n_bl, n_ch,
    lm_ref, owner_ref, freq_ref, pos_ref, pairs_ref, coh_ref, vis_ref, beam_ref,
    res_ref, gains_ref,
    pairs_in, coh_in, vis_in, beam_in, hot, model, part, part_in, total, full, pair, res_out, res_in,
    ex_send, ex_recv, sum_send, sum_recv, all_send, all_recv, back_send, back_recv,
):
    k = freq_ref.shape[0]
    nb_loc = pairs_ref.shape[1]
    nb = nb_loc * n_bl
    n = n_bl * n_ch
    stations = pos_ref.shape[1]
    slot_dev = coh_ref.shape[1]
    my_bl, my_ch = lax.axis_index("bl"), lax.axis_index("ch")
    me = my_bl * n_ch + my_ch

    def peer(off):
        return lax.rem(me + off, n)

    def place(p):
        return {"bl": lax.div(p, n_ch), "ch": lax.rem(p, n_ch)}

    barrier = pltpu.get_barrier_semaphore()

    def greet(off, _):
        pl.semaphore_signal(barrier, inc=1, device_id=place(peer(off)), device_id_type=pl.DeviceIdType.MESH)
        return 0

    lax.fori_loop(1, n, greet, 0)
    pl.semaphore_wait(barrier, n - 1)

    def source(kind, to):
        if kind == 0:
            return pairs_ref
        if kind == 1:
            return coh_ref.at[to]
        if kind == 2:
            return vis_ref.at[:, to]
        return beam_ref.at[kind - 3, :, to]

    def landing(kind, frm):
        if kind == 0:
            return pairs_in.at[frm]
        if kind == 1:
            return coh_in.at[frm]
        if kind == 2:
            return vis_in.at[frm]
        return beam_in.at[kind - 3, frm]

    def own(kind):
        return pltpu.make_async_copy(source(kind, my_bl), landing(kind, my_bl), ex_recv.at[kind, my_bl])

    def exchange(kind, to, frm):
        return pltpu.make_async_remote_copy(
            src_ref=source(kind, to),
            dst_ref=landing(kind, frm),
            send_sem=ex_send.at[kind, to],
            recv_sem=ex_recv.at[kind, frm],
            device_id={"bl": to},
            device_id_type=pl.DeviceIdType.MESH,
        )

    kinds = 3 + DIRS

    def send_out(kind):
        for off in range(1, n_bl):
            exchange(kind, lax.rem(my_bl + off, n_bl), my_bl).start()
        own(kind).start()

    for kind in range(3 + WINDOW):
        send_out(kind)

    def arrived(kind):
        own(kind).wait()
        for off in range(1, n_bl):
            frm = lax.rem(my_bl + n_bl - off, n_bl)
            exchange(kind, frm, frm).wait_recv()

    arrived(0)
    ids = lax.broadcasted_iota(jnp.int32, (stations, nb_loc), 0)
    live_parts = []
    for frm in range(n_bl):
        for side in range(2):
            at = side * nb + frm * nb_loc
            hot[:, at : at + nb_loc] = jnp.where(
                ids == pairs_in[frm, side : side + 1, :], 1.0, 0.0
            ).astype(jnp.bfloat16)
        live_parts.append(
            jnp.where(pairs_in[frm, 0:1, :] != pairs_in[frm, 1:2, :], 1.0, 0.0)
        )
    live = jnp.concatenate(live_parts, axis=1)
    at = look_up(pos_ref[...], hot[...], 3)
    apart = at[:, :nb] - at[:, nb:]
    freq = freq_ref[...]
    eye = lax.broadcasted_iota(jnp.int32, (k, k), 0) == lax.broadcasted_iota(jnp.int32, (k, k), 1)

    def put_row(d, i, value):
        line = jnp.sum(value, axis=0, keepdims=True)
        for j in range(n_bl):
            part[d][j, i : i + 1, :] = line[:, j * nb_loc : (j + 1) * nb_loc]

    def get_row(d, i):
        return jnp.concatenate([full[d][j, i : i + 1, :] for j in range(n_bl)], axis=1)

    arrived(1)
    arrived(2)
    vis = [jnp.concatenate([vis_in[frm, c] for frm in range(n_bl)], axis=1) for c in range(2)]
    def make_model(d):
        turns = freq * (apart[0:1] * lm_ref[d, 0] + apart[1:2] * lm_ref[d, 1])
        cosine, sine = phasor(turns)
        line = jnp.zeros((1, k), jnp.float32)
        for r in range(n_bl * slot_dev):
            line = line + jnp.where(
                owner_ref[d] == r, coh_in[r // slot_dev, r % slot_dev : r % slot_dev + 1, :], 0.0
            )
        flux = jnp.sum(jnp.where(eye, line, 0.0), axis=1, keepdims=True)
        scale = flux * live
        arrived(3 + d)
        if d + WINDOW < DIRS:
            send_out(3 + d + WINDOW)
        e = jnp.concatenate(
            [
                jnp.concatenate([beam_in[d, frm, c] for frm in range(n_bl)], axis=1)
                for c in range(2)
            ],
            axis=0,
        )
        both = look_up(e, hot[...], 2)
        left_r, right_r = both[:k, :nb], both[:k, nb:]
        left_i, right_i = both[k:, :nb], both[k:, nb:]
        cross_r = left_r * right_r + left_i * right_i
        cross_i = left_i * right_r - left_r * right_i
        m_r = (cross_r * cosine - cross_i * sine) * scale
        m_i = (cross_r * sine + cross_i * cosine) * scale
        model[d, 0] = m_r
        model[d, 1] = m_i
        put_row(d, 0, m_r * m_r + m_i * m_i)
        put_row(d, 1, vis[0] * m_r + vis[1] * m_i)
        put_row(d, 2, vis[1] * m_r - vis[0] * m_i)
        for f in range(d):
            o_r, o_i = model[f, 0], model[f, 1]
            put_row(d, 3 + 2 * f, o_r * m_r + o_i * m_i)
            put_row(d, 4 + 2 * f, o_i * m_r - o_r * m_i)

    def share(d, to_bl):
        owner = to_bl * n_ch + d % n_ch
        slot = lax.rem(me - owner + n, n) - 1
        return pltpu.make_async_remote_copy(
            src_ref=part[d].at[to_bl],
            dst_ref=part_in[d].at[slot],
            send_sem=sum_send.at[d],
            recv_sem=sum_recv.at[d],
            device_id={"bl": to_bl, "ch": d % n_ch},
            device_id_type=pl.DeviceIdType.MESH,
        )

    def spread(d, p):
        return pltpu.make_async_remote_copy(
            src_ref=total[d],
            dst_ref=full[d].at[my_bl],
            send_sem=all_send.at[d],
            recv_sem=all_recv.at[d],
            device_id=place(p),
            device_id_type=pl.DeviceIdType.MESH,
        )

    def wait_for(ref, count, sem):
        block = ref.at[pl.ds(0, count)]
        pltpu.make_async_copy(block, block, sem).wait()

    def start_share(d):
        for off in range(1, n_bl):
            share(d, lax.rem(my_bl + off, n_bl)).start()

        @pl.when(my_ch != d % n_ch)
        def _():
            share(d, my_bl).start()

    def reduce_and_spread(d):
        @pl.when(my_ch == d % n_ch)
        def _():
            wait_for(part_in[d], n - 1, sum_recv.at[d])
            value = jnp.sum(part_in[d][...], axis=0) + part[d][my_bl]
            total[d][...] = value

            def step(off, _):
                spread(d, peer(off)).start()
                return 0

            lax.fori_loop(1, n, step, 0)
            full[d][my_bl] = value

    def sums_arrived(d):
        @pl.when(my_ch == d % n_ch)
        def _():
            if n_bl > 1:
                wait_for(full[d], n_bl - 1, all_recv.at[d])

        @pl.when(my_ch != d % n_ch)
        def _():
            wait_for(full[d], n_bl, all_recv.at[d])

    def sums_sent(d):
        @pl.when(my_ch == d % n_ch)
        def _():
            if n_bl > 1:
                wait_for(part[d], n_bl - 1, sum_send.at[d])
            wait_for(part_in[d], n - 1, all_send.at[d])

        @pl.when(my_ch != d % n_ch)
        def _():
            wait_for(part[d], n_bl, sum_send.at[d])

    def solve(d):
        sums_arrived(d)
        q, p_r, p_i = get_row(d, 0), get_row(d, 1), get_row(d, 2)
        for f in range(d):
            b_r, b_i = get_row(d, 3 + 2 * f), get_row(d, 4 + 2 * f)
            g_r, g_i = pair[2 * f : 2 * f + 1], pair[2 * f + 1 : 2 * f + 2]
            p_r = p_r - (g_r * b_r - g_i * b_i)
            p_i = p_i - (g_r * b_i + g_i * b_r)
        first = add_up(
            jnp.concatenate(
                [
                    jnp.concatenate([p_r, p_r], axis=1),
                    jnp.concatenate([p_i, -p_i], axis=1),
                    jnp.concatenate([q, q], axis=1),
                ],
                axis=0,
            ),
            hot[...],
            3,
        )
        w = first[2:3]
        scale = 0.5 / (w + MIXING * w + 1.0)
        gain_r = 0.5 + (first[0:1] + MIXING * w + 1.0) * scale
        gain_i = first[1:2] * scale
        at = look_up(jnp.concatenate([gain_r, gain_i], axis=0), hot[...], 3)
        near_r, far_r = at[0:1, :nb], at[0:1, nb:]
        near_i, far_i = at[1:2, :nb], at[1:2, nb:]
        head = [p_r * far_r - p_i * far_i, p_r * far_i + p_i * far_r, q * (far_r * far_r + far_i * far_i)]
        tail = [p_r * near_r + p_i * near_i, p_r * near_i - p_i * near_r, q * (near_r * near_r + near_i * near_i)]
        second = add_up(
            jnp.concatenate([jnp.concatenate([h, t], axis=1) for h, t in zip(head, tail)], axis=0),
            hot[...],
            3,
        )
        scale = 0.5 / (second[2:3] + MIXING * w + 1.0)
        gain_r = 0.5 * gain_r + (second[0:1] + MIXING * w + 1.0) * scale
        gain_i = 0.5 * gain_i + second[1:2] * scale
        gains = jnp.concatenate([gain_r, gain_i], axis=0)
        gains_ref[d] = gains
        at = look_up(gains, hot[...], 3)
        near_r, far_r = at[0:1, :nb], at[0:1, nb:]
        near_i, far_i = at[1:2, :nb], at[1:2, nb:]
        pair[2 * d : 2 * d + 1] = near_r * far_r + near_i * far_i
        pair[2 * d + 1 : 2 * d + 2] = near_i * far_r - near_r * far_i

    def take_off(j, dirs, r_r, r_i):
        lo, hi = j * nb_loc, (j + 1) * nb_loc
        for d in dirs:
            g_r, g_i = pair[2 * d : 2 * d + 1, lo:hi], pair[2 * d + 1 : 2 * d + 2, lo:hi]
            m_r, m_i = model[d, 0, :, lo:hi], model[d, 1, :, lo:hi]
            r_r = r_r - (g_r * m_r - g_i * m_i)
            r_i = r_i - (g_r * m_i + g_i * m_r)
        res_out[j, 0] = r_r
        res_out[j, 1] = r_i

    for step in range(DIRS - 1 + LAG):
        if step < DIRS:
            make_model(step)
            start_share(step)
        if step >= LAG:
            solve(step - LAG)
        if 1 <= step <= DIRS:
            reduce_and_spread(step - 1)
    for j in range(n_bl):
        take_off(j, range(DIRS - 1), vis_in[j, 0], vis_in[j, 1])
    solve(DIRS - 1)
    for j in range(n_bl):
        take_off(j, range(DIRS - 1, DIRS), res_out[j, 0], res_out[j, 1])

    def back(to, slot):
        return pltpu.make_async_remote_copy(
            src_ref=res_out.at[to],
            dst_ref=res_in.at[slot],
            send_sem=back_send.at[to],
            recv_sem=back_recv.at[slot],
            device_id={"bl": to},
            device_id_type=pl.DeviceIdType.MESH,
        )

    for off in range(1, n_bl):
        back(lax.rem(my_bl + off, n_bl), my_bl).start()
    res_in[my_bl] = res_out[my_bl]
    for off in range(1, n_bl):
        frm = lax.rem(my_bl + n_bl - off, n_bl)
        back(frm, frm).wait_recv()
    for j in range(n_bl):
        for c in range(2):
            res_ref[c, j] = res_in[j, c]

    for kind in range(kinds):
        for off in range(1, n_bl):
            to = lax.rem(my_bl + off, n_bl)
            exchange(kind, to, to).wait_send()
    for d in range(DIRS):
        sums_sent(d)
    for off in range(1, n_bl):
        to = lax.rem(my_bl + off, n_bl)
        back(to, to).wait_send()


def on_device(n_bl, n_ch, visibilities, beam, coherency, owner, positions, direction_lm, pairs):
    chans = visibilities.shape[2]
    k = chans // n_bl
    stations = positions.shape[1]
    st_loc = beam.shape[4]
    nb_loc = pairs.shape[1]
    nb = nb_loc * n_bl
    slot_dev = coherency.shape[0]
    n = n_bl * n_ch
    rows = [3 + 2 * d for d in range(DIRS)]
    start = lax.axis_index("ch") * chans + lax.axis_index("bl") * k
    freq = 1.0 + 0.5 * (start + jnp.arange(k)).astype(jnp.float32)[:, None] / NC
    coh = coherency[:, 0].reshape(slot_dev, n_bl, k).transpose(1, 0, 2)
    vis = visibilities.reshape(2, n_bl, k, nb_loc)
    beams = beam.reshape(DIRS, 2, n_bl, k, st_loc)
    vmem = pl.BlockSpec(memory_space=pltpu.VMEM)
    smem = pl.BlockSpec(memory_space=pltpu.SMEM)
    anywhere = pl.BlockSpec(memory_space=pl.ANY)
    f32 = jnp.float32
    dma = pltpu.SemaphoreType.DMA
    res, gains = pl.pallas_call(
        functools.partial(one_kernel, n_bl, n_ch),
        out_shape=(
            jax.ShapeDtypeStruct((2, n_bl, k, nb_loc), f32),
            jax.ShapeDtypeStruct((DIRS, 2, stations), f32),
        ),
        in_specs=[smem, smem, vmem, vmem, vmem, vmem, anywhere, anywhere],
        out_specs=(vmem, vmem),
        scratch_shapes=[
            pltpu.VMEM((n_bl, 2, nb_loc), jnp.int32),
            pltpu.VMEM((n_bl, slot_dev, k), f32),
            pltpu.VMEM((n_bl, 2, k, nb_loc), f32),
            pltpu.VMEM((DIRS, n_bl, 2, k, st_loc), f32),
            pltpu.VMEM((stations, 2 * nb), jnp.bfloat16),
            pltpu.VMEM((DIRS, 2, k, nb), f32),
            [pltpu.VMEM((n_bl, r, nb_loc), f32) for r in rows],
            [pltpu.VMEM((n - 1, r, nb_loc), f32) for r in rows],
            [pltpu.VMEM((r, nb_loc), f32) for r in rows],
            [pltpu.VMEM((n_bl, r, nb_loc), f32) for r in rows],
            pltpu.VMEM((2 * DIRS, nb), f32),
            pltpu.VMEM((n_bl, 2, k, nb_loc), f32),
            pltpu.VMEM((n_bl, 2, k, nb_loc), f32),
            dma((3 + DIRS, n_bl)),
            dma((3 + DIRS, n_bl)),
            dma((DIRS,)),
            dma((DIRS,)),
            dma((DIRS,)),
            dma((DIRS,)),
            dma((n_bl,)),
            dma((n_bl,)),
        ],
        compiler_params=pltpu.CompilerParams(
            collective_id=0, has_side_effects=True, vmem_limit_bytes=VMEM_LIMIT
        ),
        name="peel",
    )(direction_lm, owner, freq, positions, pairs, coh, vis, beams)
    return (res.reshape(2, 1, chans, nb_loc), gains[:, :, None])


def solution(mesh):
    return jax.shard_map(
        functools.partial(on_device, mesh.shape["bl"], mesh.shape["ch"]),
        mesh=mesh,
        in_specs=(
            P(None, "pol", "ch", ("grp", "bl")),
            P("grp", None, "pol", "ch", "bl"),
            P(("grp", "bl"), "pol", "ch"),
            P("grp"),
            P(None, "grp"),
            P("grp", None),
            P(None, ("grp", "bl")),
        ),
        out_specs=(P(None, "pol", "ch", ("grp", "bl")), P("grp", None, "pol", None)),
        check_vma=False,
    )
```
